32 devices in a mesh: frame: 8 (over y, x, core), head: 4 (over z).
Axes of the slice: x: 2, y: 2, z: 4, core: 2. Of those that a mesh axis runs over, the one named last changes fastest.
Arguments:
- queries: bfloat16 [16384, 512], P('frame', 'head'), may hold values from -64 to 64
- keys: bfloat16 [16384, 512], P('frame', 'head'), may hold values from -4 to 4
- values: bfloat16 [16384, 512], P('frame', 'head'), may hold values from -6 to 6
- block_mask: int32 [4, 8, 32, 45], P('head', 'frame'), may hold values 0 or 1
- out_weight: bfloat16 [512, 3072], P('head'), may hold values from -2 to 2
Outputs:
- projected: bfloat16 [16384, 3072], P(('frame', 'head'))
The draws below stay inside these ranges and needn't reach their ends.
All inputs are finite; a program needn't handle non-finite values. No bound on the sum of `block_mask` on one device may be relied on, other than what follows from the above.
Results may differ from the reference program's by a relative error of at most 0.018.
Values may be sent and summed in bfloat16 or wider, within the bound.
No kernel may reach another device: no remote copies, remote signals or barrier semaphores. Data moves between devices by JAX's collectives and lax.ppermute only.
A program may use at most 128 MiB of HBM per device.

```python
import math
import jax
import jax.numpy as jnp
from jax import lax

D = 3072
HEAD_DIM = 128
HEADS = 4
TROWS = 4
TCOLS = 8
WIN = 45
TILE = 64
FRAMES = 8
TOKENS = 16384


def shared_pair(key):
    width = HEADS * HEAD_DIM
    key_base = jnp.clip(jax.random.normal(jax.random.fold_in(key, 11), (TOKENS, width), jnp.float32), -4.0, 4.0)
    query_base = jnp.clip(2.0 * jax.random.normal(jax.random.fold_in(key, 12), (TOKENS, width), jnp.float32), -8.0, 8.0)
    return (query_base, key_base)


def draw_queries(key, part):
    query_base, key_base = shared_pair(key)
    return query_base.astype(jnp.bfloat16)


def draw_keys(key, part):
    query_base, key_base = shared_pair(key)
    return key_base.astype(jnp.bfloat16)


def plant(values, stream_key, smallest, high):
    longest = values.shape.index(max(values.shape))
    spots = []
    for shift in (0, 1):
        where = [jax.random.randint(jax.random.fold_in(stream_key, axis), (), 0, length) for axis, length in enumerate(values.shape)]
        where[longest] = (where[longest] + shift) % values.shape[longest]
        spots.append(tuple(where))
    return values.at[spots[0]].set(smallest).at[spots[1]].set(high)


def levels(rng, extent, pieces, smallest, largest):
    loudness, own = 1.0, jax.random.fold_in(rng, 6)
    for position, shards_of in pieces:
        draws = jnp.exp(jax.random.uniform(jax.random.fold_in(own, position), (shards_of,), jnp.float32, smallest / len(pieces), largest / len(pieces)))
        loudness = loudness * jnp.repeat(draws, extent[position] // shards_of).reshape([-1 if axis == position else 1 for axis in range(len(extent))])
    return loudness


def centred(key, dims, spread, reach, split=(), held_as=jnp.bfloat16):
    gain = levels(key, dims, split, -0.22, 0.18) if split else 1.0
    array = jax.random.normal(key, dims, jnp.float32) * spread * gain
    return jnp.minimum(jnp.maximum(array, -reach), reach).astype(held_as)


def setup_inputs(seed: int = 0) -> dict:
    arg_keys = jax.random.split(jax.random.key(seed), 6)
    queries = draw_queries(jax.random.fold_in(arg_keys[5], 71), 0)
    keys = draw_keys(jax.random.fold_in(arg_keys[5], 71), 0)
    values = centred(arg_keys[2], (TOKENS, HEADS * HEAD_DIM), 1.0, 6.0, ((0, 8), (1, 4)))
    block_mask = plant((jax.random.randint(arg_keys[3], (HEADS, FRAMES, TROWS * TCOLS, WIN), 0, 4) < 3).astype(jnp.int32), jax.random.fold_in(arg_keys[3], 1), 0, 1)
    out_weight = centred(arg_keys[4], (HEADS * HEAD_DIM, D), (HEADS * HEAD_DIM // 64) ** -0.5, 2.0, ((0, 4),))
    return dict(queries=queries, keys=keys, values=values, block_mask=block_mask, out_weight=out_weight)


def tile_allowed(mask_rows, frame, row, frames_total):
    frame_step = jnp.arange(3, dtype=jnp.int32)[None, :, None, None]
    row_step = jnp.arange(3, dtype=jnp.int32)[None, None, :, None]
    query_col = jnp.arange(TCOLS, dtype=jnp.int32)[:, None, None, None]
    key_col = jnp.arange(TCOLS, dtype=jnp.int32)[None, None, None, :]
    col_step = key_col - query_col
    offset = frame_step * 15 + row_step * 5 + col_step + 2
    picked = offset[..., None] == jnp.arange(WIN, dtype=jnp.int32)
    chosen = lax.optimization_barrier(jnp.sum(jnp.where(picked, mask_rows[:, None, None, None, :], 0), axis=-1)) > 0
    centre = (frame_step == 1) & (row_step == 1) & (col_step == 0)
    key_frame = frame + frame_step - 1
    key_row = row + row_step - 1
    inside = (key_frame >= 0) & (key_frame < frames_total) & (key_row >= 0) & (key_row < TROWS)
    nearby = jnp.abs(col_step) <= 2
    allowed = (chosen | centre) & nearby & inside
    expanded = jnp.broadcast_to(allowed[:, None, :, :, :, None], (TCOLS, TILE, 3, 3, TCOLS, TILE))
    return expanded.reshape(TCOLS * TILE, 9 * TCOLS * TILE)

def attend_block(query_block, key_block, value_block, allowed):
    scale = 1.0 / math.sqrt(HEAD_DIM)
    scores = jnp.dot(query_block, key_block.T, preferred_element_type=jnp.float32) * scale
    scores = jnp.where(allowed, scores, -jnp.inf)
    peak = lax.optimization_barrier(jnp.max(scores, axis=1, keepdims=True))
    expos = jnp.exp(scores - peak)
    weights = (expos / lax.optimization_barrier(jnp.sum(expos, axis=1, keepdims=True))).astype(jnp.bfloat16)
    return jnp.dot(weights, value_block, preferred_element_type=jnp.float32).astype(jnp.bfloat16)

def reference(queries, keys, values, block_mask, out_weight):
    span = TCOLS * TILE
    query_grid = queries.reshape(FRAMES, TROWS, span, HEADS, HEAD_DIM)
    pair = jnp.stack([keys, values]).reshape(2, FRAMES, TROWS, span, HEADS, HEAD_DIM)
    padded = jnp.pad(pair, ((0, 0), (1, 1), (1, 1), (0, 0), (0, 0), (0, 0)))
    mask_grid = block_mask.reshape(HEADS, FRAMES, TROWS, TCOLS, WIN)

    def one_block(which):
        head = (which // (FRAMES * TROWS)).astype(jnp.int32)
        frame = (which // TROWS % FRAMES).astype(jnp.int32)
        row = (which % TROWS).astype(jnp.int32)
        zero = jnp.zeros((), jnp.int32)
        query_block = lax.dynamic_slice(query_grid, (frame, row, zero, head, zero), (1, 1, span, 1, HEAD_DIM)).reshape(span, HEAD_DIM)
        pair_block = lax.dynamic_slice(padded, (zero, frame, row, zero, head, zero), (2, 3, 3, span, 1, HEAD_DIM)).reshape(2, 9 * span, HEAD_DIM)
        mask_rows = lax.dynamic_slice(mask_grid, (head, frame, row, zero, zero), (1, 1, 1, TCOLS, WIN)).reshape(TCOLS, WIN)
        allowed = tile_allowed(mask_rows, frame, row, FRAMES)
        return attend_block(query_block, pair_block[0], pair_block[1], allowed)
    blocks = lax.map(one_block, jnp.arange(HEADS * FRAMES * TROWS, dtype=jnp.int32))
    attention = blocks.reshape(HEADS, FRAMES, TROWS, span, HEAD_DIM).transpose(1, 2, 3, 0, 4).reshape(TOKENS, HEADS * HEAD_DIM)
    return jnp.dot(attention, out_weight, preferred_element_type=jnp.float32).astype(jnp.bfloat16)
```

```python
import functools
import math

import jax
import jax.numpy as jnp
from jax import lax
from jax.experimental import pallas as pl
from jax.experimental.pallas import tpu as pltpu
from jax.sharding import PartitionSpec as P

HEAD_DIM = 128
TROWS = 4
TCOLS = 8
WIN = 45
TILE = 64
SPAN = TCOLS * TILE
HALF = SPAN // 2
KEYS = 6 * TILE
SHIFT = 2 * TILE
FAR = -(2.0**100)
RATE = math.log2(math.e) / math.sqrt(HEAD_DIM)


def fill_bias(mask_ref, padded_ref, bias_ref, step, frame_inside):
    padded_ref[...] = jnp.zeros_like(padded_ref)
    padded_ref[:, :WIN] = mask_ref[...]
    col = lax.broadcasted_iota(jnp.int32, (TCOLS, 128), 0)
    key_col = lax.broadcasted_iota(jnp.int32, (TCOLS, 128), 1)
    near = jnp.abs(key_col - col) <= 2
    for r in range(TROWS):
        rows = pltpu.roll(padded_ref[r * TCOLS : (r + 1) * TCOLS, :], 0, 1, stride=1, stride_axis=0)
        for b in range(3):
            if not 0 <= r + b - 1 < TROWS:
                continue
            picked = [pltpu.roll(rows, 128 - (15 * a + 5 * b + 2), 1) for a in range(3)]
            chosen = jnp.where(step == 0, picked[0], jnp.where(step == 1, picked[1], picked[2])) > 0
            if b == 1:
                chosen = chosen | ((key_col == col) & (step == 1))
            allowed = chosen & near & frame_inside
            bias = jnp.where(allowed, 0.0, FAR).astype(jnp.float32)
            for c in range(TCOLS):
                start = (r * 3 + b) * SPAN + c * TILE
                bias_ref[start : start + TILE, :] = jnp.broadcast_to(bias[c : c + 1, :], (TILE, 128)).astype(
                    jnp.bfloat16
                )


def attend_kernel(which, first, last, count, frame_axis, *refs):
    refs = list(refs)
    q_ref, k_ref, v_ref, mask_ref = refs[:4]
    refs = refs[4:]
    if not first:
        peak_in, total_in, acc_in = refs[:3]
        refs = refs[3:]
    if last:
        out_ref = refs.pop(0)
    else:
        peak_out, total_out, acc_out = refs[:3]
        refs = refs[3:]
    padded_ref, bias_ref = refs
    frame = lax.axis_index(frame_axis)
    if which == "own":
        step = jnp.int32(1)
    elif which == "chip":
        step = 2 - 2 * (frame % 2)
    else:
        step = 2 * (frame % 2)
    key_frame = frame + step - 1
    inside = (key_frame >= 0) & (key_frame < count)
    fill_bias(mask_ref, padded_ref, bias_ref, step, inside)

    tile_of = lax.broadcasted_iota(jnp.int32, (KEYS, 128), 0) // TILE
    lane = lax.broadcasted_iota(jnp.int32, (KEYS, 128), 1)
    ones = jnp.ones((KEYS, 128), jnp.bfloat16)

    def block(row, key_row, side, rows_here):
        at = pl.multiple_of(row * SPAN + side * HALF, HALF)
        query = q_ref[pl.ds(at, HALF), :]
        marks = (lane == tile_of + side * 2).astype(jnp.float32).astype(jnp.bfloat16)
        scores = []
        for j in range(rows_here):
            b = key_row + j - row + 1
            bias = bias_ref[pl.ds(pl.multiple_of((row * 3 + b) * SPAN + side * HALF, HALF), HALF), :]
            key = k_ref[pl.ds(pl.multiple_of((key_row + j) * SPAN + side * SHIFT, SHIFT), KEYS), :]
            scores.append(
                lax.dot_general(
                    jnp.concatenate([query, bias], axis=1),
                    jnp.concatenate([key, marks], axis=1),
                    (((1,), (1,)), ((), ())),
                    preferred_element_type=jnp.float32,
                )
            )
        peak = functools.reduce(jnp.maximum, scores)
        peak = jnp.max(peak, axis=1, keepdims=True)
        if not first:
            before = peak_in[pl.ds(at, HALF), :][:, :1]
            peak = jnp.maximum(peak, before)
        acc = None
        for j in range(rows_here):
            expo = jnp.exp2((scores[j] - peak) * RATE).astype(jnp.bfloat16)
            value = v_ref[pl.ds(pl.multiple_of((key_row + j) * SPAN + side * SHIFT, SHIFT), KEYS), :]
            part = jnp.dot(expo, jnp.concatenate([value, ones], axis=1), preferred_element_type=jnp.float32)
            acc = part if acc is None else acc + part
        total = acc[:, 128:]
        acc = acc[:, :128]
        if not first:
            fade = jnp.exp2((before - peak) * RATE)
            total = total + fade * total_in[pl.ds(at, HALF), :]
            acc = acc + fade * acc_in[pl.ds(at, HALF), :]
        if last:
            out_ref[pl.ds(at, HALF), :] = (acc / total).astype(jnp.bfloat16)
        else:
            peak_out[pl.ds(at, HALF), :] = jnp.broadcast_to(peak, (HALF, 128))
            total_out[pl.ds(at, HALF), :] = total
            acc_out[pl.ds(at, HALF), :] = acc

    def inner(i, carry):
        row = 1 + i // 2
        block(row, row - 1, i % 2, 3)
        return carry

    def border(i, carry):
        far = i // 2
        block(far * (TROWS - 1), far * (TROWS - 2), i % 2, 2)
        return carry

    lax.fori_loop(0, 4, inner, 0)
    lax.fori_loop(0, 4, border, 0)


def attend(which, queries, keys, values, mask, state, last, count):
    tokens = queries.shape[0]
    first = state is None
    full = jax.ShapeDtypeStruct((tokens, 128), jnp.float32)
    out = jax.ShapeDtypeStruct((tokens, HEAD_DIM), jnp.bfloat16) if last else (full, full, full)
    args = (queries, keys, values, mask) + (() if first else tuple(state))
    vmem = pl.BlockSpec(memory_space=pltpu.VMEM)
    return pl.pallas_call(
        functools.partial(attend_kernel, which, first, last, count, "frame"),
        out_shape=out,
        in_specs=[vmem] * len(args),
        out_specs=vmem if last else (vmem,) * 3,
        scratch_shapes=[
            pltpu.VMEM((TROWS * TCOLS, 128), jnp.int32),
            pltpu.VMEM((TROWS * 3 * SPAN, 128), jnp.bfloat16),
        ],
        compiler_params=pltpu.CompilerParams(vmem_limit_bytes=40 * 1024 * 1024),
        cost_estimate=pl.CostEstimate(flops=2_000_000_000, bytes_accessed=4_000_000, transcendentals=2_000_000),
        name="attend_" + which,
    )(*args)


def swap(block, axis, bit):
    count = lax.axis_size(axis)
    return lax.ppermute(block, axis, [(i, i ^ bit) for i in range(count)])


def on_device(queries, keys, values, block_mask, out_weight):
    frames = lax.axis_size("frame")
    heads = lax.axis_size("head")
    frame = lax.axis_index("frame")
    head = lax.axis_index("head")
    mask = block_mask.reshape(TROWS * TCOLS, WIN)
    pair = jnp.stack([keys, values])
    odd = [(i, i + 1) for i in range(1, frames - 1, 2)]
    far = lax.ppermute(pair, "frame", odd + [(j, i) for i, j in odd])
    near = swap(pair, "frame", 1)

    depth = out_weight.shape[0]
    quarter = depth // 4
    y = frame // (frames // 2)
    mine = lax.dynamic_slice_in_dim(out_weight, (2 * y + frame % 2) * quarter, quarter, 0)
    pieces = jnp.stack([swap(mine, "head", s) for s in range(1, heads)])
    other = swap(pieces, "frame", frames // 2)
    low, high = jnp.where(y == 0, pieces, other), jnp.where(y == 0, other, pieces)
    both = jnp.stack([low, high], axis=1)
    beside = swap(both, "frame", 1)
    even = frame % 2 == 0
    first, second = jnp.where(even, both, beside), jnp.where(even, beside, both)
    whole = jnp.stack([first, second], axis=2).reshape(heads - 1, depth, -1)
    whole = jnp.concatenate([out_weight[None], whole]).reshape(heads * depth, -1)

    state = attend("own", queries, keys, values, mask, None, False, frames)
    state = attend("chip", queries, near[0], near[1], mask, state, False, frames)
    done = attend("far", queries, far[0], far[1], mask, state, True, frames)

    tokens = queries.shape[0] // heads
    rows = done.reshape(heads, tokens, HEAD_DIM)
    parts = [lax.dynamic_index_in_dim(rows, head, 0, False)]
    for s in range(1, heads):
        parts.append(swap(lax.dynamic_index_in_dim(rows, head ^ s, 0, False), "head", s))
    attention = jnp.concatenate(parts, axis=1)
    return jnp.dot(attention, whole, preferred_element_type=jnp.float32).astype(jnp.bfloat16)


def solution(mesh):
    return jax.shard_map(
        on_device,
        mesh=mesh,
        in_specs=(
            P("frame", "head"),
            P("frame", "head"),
            P("frame", "head"),
            P("head", "frame", None, None),
            P("head", None),
        ),
        out_specs=P(("frame", "head"), None),
        check_vma=False,
    )
```

```python
import functools
import math

import jax
import jax.numpy as jnp
from jax import lax
from jax.experimental import pallas as pl
from jax.experimental.pallas import tpu as pltpu
from jax.sharding import PartitionSpec as P

HEAD_DIM = 128
TROWS = 4
TCOLS = 8
WIN = 45
TILE = 64
SPAN = TCOLS * TILE
HALF = SPAN // 2
KEYS = 6 * TILE
SHIFT = 2 * TILE
PAIR = 2 * SPAN
FAR = -(2.0**100)
RATE = math.log2(math.e) / math.sqrt(HEAD_DIM)
BIAS_SHAPE = (TROWS * 3 * SPAN, 128)
VMEM_BYTES = 10 * 1024 * 1024
GATE_FLOPS = 20_000_000_000


def keep(block):
    return pltpu.with_memory_space_constraint(block, pltpu.VMEM)


def stay(block):
    return pltpu.with_memory_space_constraint(block, pltpu.HBM)


def fill_bias(mask_ref, padded_ref, frame, frames, bias_refs):
    padded_ref[...] = jnp.zeros_like(padded_ref)
    padded_ref[: TROWS * TCOLS, :WIN] = mask_ref[...].astype(jnp.float32)
    turned = padded_ref[...].T
    key_col = lax.broadcasted_iota(jnp.int32, (TCOLS, 128), 0)
    step = key_col - lax.broadcasted_iota(jnp.int32, (TCOLS, 128), 1)
    odd = frame % 2
    for r in range(TROWS):
        windows = turned if r == 0 else pltpu.roll(turned, 128 - r * TCOLS, 1)
        for b in range(3):
            if not 0 <= r + b - 1 < TROWS:
                continue
            picked = []
            for a in range(3):
                base = 15 * a + 5 * b + 2
                chosen = jnp.zeros((TCOLS, 128), jnp.float32)
                for d in range(-2, 3):
                    chosen = jnp.where(step == d, jnp.broadcast_to(windows[base + d : base + d + 1, :], (TCOLS, 128)), chosen)
                picked.append(chosen > 0)
            own = picked[1] | (step == 0) if b == 1 else picked[1]
            low = jnp.where(picked[0] & (frame > 0), 0.0, FAR)
            high = jnp.where(picked[2] & (frame < frames - 1), 0.0, FAR)
            for ref, bias in zip(
                bias_refs,
                (jnp.where(own, 0.0, FAR), jnp.where(odd == 1, low, high), jnp.where(odd == 1, high, low)),
            ):
                for k in range(TCOLS):
                    start = (r * 3 + b) * SPAN + k * TILE
                    ref[start : start + TILE, :] = jnp.broadcast_to(bias[k : k + 1, :], (TILE, 128)).astype(
                        jnp.bfloat16
                    )


def fill_marks(marks_ref):
    tile = lax.broadcasted_iota(jnp.int32, (SPAN, 128), 0) // TILE
    lane = lax.broadcasted_iota(jnp.int32, (SPAN, 128), 1)
    marks_ref[...] = (lane == tile).astype(jnp.float32).astype(jnp.bfloat16)


def attend_block(query, pieces, before):
    keys = jnp.concatenate([jnp.concatenate([key, bias], axis=1) for key, bias, _ in pieces], axis=0)
    values = jnp.concatenate([value for _, _, value in pieces], axis=0)
    values = jnp.concatenate([values, jnp.ones_like(values)], axis=1)
    scores = lax.dot_general(query, keys, (((1,), (1,)), ((), ())), preferred_element_type=jnp.float32)
    peak = jnp.max(scores, axis=1, keepdims=True)
    if before is not None:
        peak = jnp.maximum(peak, before[0][:, :1])
    expo = jnp.exp2((scores - peak) * RATE).astype(jnp.bfloat16)
    acc = jnp.dot(expo, values, preferred_element_type=jnp.float32)
    total, acc = acc[:, HEAD_DIM:], acc[:, :HEAD_DIM]
    if before is not None:
        fade = jnp.exp2((before[0] - peak) * RATE)
        total = total + fade * before[1]
        acc = acc + fade * before[2]
    return peak, total, acc


def flipped(row, flip, rows):
    return row + flip * (rows - 1 - 2 * row)


class Layout:
    def __init__(self, flip, q_ref, bias_ref, marks_ref):
        self.flip, self.q, self.bias, self.marks = flip, q_ref, bias_ref, marks_ref

    def query(self, row, side):
        at = pl.multiple_of(flipped(row, self.flip, TROWS) * SPAN + side * HALF, HALF)
        return jnp.concatenate([self.q[pl.ds(at, HALF), :], self.marks[side * HALF : (side + 1) * HALF, :]], axis=1)

    def piece(self, row, key_row, side, k_ref, v_ref, at_row):
        r, kr = flipped(row, self.flip, TROWS), flipped(key_row, self.flip, TROWS)
        at = pl.multiple_of((r * 3 + kr - r + 1) * SPAN + side * SHIFT, SHIFT)
        start = pl.multiple_of(at_row * SPAN + side * SHIFT, SHIFT)
        return (
            k_ref[pl.ds(start, KEYS), :],
            self.bias[pl.ds(at, KEYS), :],
            v_ref[pl.ds(start, KEYS), :],
        )


    def both(self, row, side, half0, half1):
        pieces = []
        for kr in around(row):
            half = (half0, half1)[kr // 2]
            pieces.append(self.piece(row, kr, side, half.at[0], half.at[1], flipped(kr % 2, self.flip, 2)))
        return pieces


def around(row):
    return range(max(row - 1, 0), min(row + 1, TROWS - 1) + 1)


def put(refs, at, state):
    for ref, value in zip(refs, state):
        ref[at : at + HALF, :] = jnp.broadcast_to(value, (HALF, 128))


def get(refs, at):
    return [ref[at : at + HALF, :] for ref in refs]


def flip_here(tuned):
    return (lax.axis_index("head") < lax.axis_size("head") // 2).astype(jnp.int32) if tuned else jnp.int32(0)


def start_all(copies):
    for copy in copies:
        copy.start()
    return copies


def pack_kernel(tuned, k_ref, v_ref, weight_ref, q_hbm, mask_hbm, first_ref, second_ref, mine_ref, q_ref, mask_ref, sems):
    flip = flip_here(tuned)
    quarter = mine_ref.shape[0]
    frame = lax.axis_index("frame")
    part = 2 * (frame // (lax.axis_size("frame") // 2)) + frame % 2
    row = pl.multiple_of(part * quarter, quarter)
    moves = []
    for i, out in enumerate((first_ref, second_ref)):
        start = pl.multiple_of((flip if i == 0 else 1 - flip) * PAIR, PAIR)
        moves += [(source.at[pl.ds(start, PAIR)], out.at[j]) for j, source in enumerate((k_ref, v_ref))]
    moves += [(weight_ref.at[pl.ds(row, quarter)], mine_ref), (q_hbm, q_ref), (mask_hbm, mask_ref)]
    for copy in start_all([pltpu.make_async_copy(a, b, sems.at[n]) for n, (a, b) in enumerate(moves)]):
        copy.wait()


def own_kernel(
    tuned,
    q_ref,
    mask_ref,
    half0,
    half1,
    again_ref,
    token_ref,
    peak,
    total,
    acc,
    bias_chip,
    bias_far,
    padded_ref,
    bias_ref,
    marks_ref,
    sem,
):
    token_ref[...] = jnp.zeros_like(token_ref)
    copy = pltpu.make_async_copy(half1, again_ref, sem)
    copy.start()
    fill_marks(marks_ref)
    fill_bias(
        mask_ref, padded_ref, lax.axis_index("frame"), lax.axis_size("frame"), (bias_ref, bias_chip, bias_far)
    )
    lay = Layout(flip_here(tuned), q_ref, bias_ref, marks_ref)
    for row in range(TROWS):
        for side in range(2):
            pieces = lay.both(row, side, half0, half1)
            put((peak, total, acc), row * SPAN + side * HALF, attend_block(lay.query(row, side), pieces, None))
    copy.wait()


def chip_kernel(
    tuned, q_ref, near0, near1, bias_ref, peak_in, total_in, acc_in, peak, total, acc, token_ref, marks_ref
):
    token_ref[...] = jnp.zeros_like(token_ref)
    fill_marks(marks_ref)
    lay = Layout(flip_here(tuned), q_ref, bias_ref, marks_ref)
    for row in range(TROWS):
        for side in range(2):
            at = row * SPAN + side * HALF
            before = get((peak_in, total_in, acc_in), at)
            state = attend_block(lay.query(row, side), lay.both(row, side, near0, near1), before)
            put((peak, total, acc), at, state)


def finish(state):
    return (state[2] / state[1]).astype(jnp.bfloat16)


def early_kernel(
    tuned, q_ref, far0, bias_ref, peak_in, total_in, acc_in, out_ref, peak, total, acc, marks_ref
):
    fill_marks(marks_ref)
    for new, old in zip((peak, total, acc), (peak_in, total_in, acc_in)):
        new[PAIR:, :] = old[3 * SPAN :, :]
    lay = Layout(flip_here(tuned), q_ref, bias_ref, marks_ref)
    for row in range(3):
        for side in range(2):
            pieces = [
                lay.piece(row, kr, side, far0.at[0], far0.at[1], flipped(kr, lay.flip, 2))
                for kr in around(row)
                if kr < 2
            ]
            at = row * SPAN + side * HALF
            state = attend_block(lay.query(row, side), pieces, get((peak_in, total_in, acc_in), at))
            if row == 0:
                out_ref[side * HALF : (side + 1) * HALF, :] = finish(state)
            else:
                put((peak, total, acc), at - SPAN, state)


def late_kernel(
    tuned,
    q_ref,
    far_ref,
    bias_ref,
    peak_in,
    total_in,
    acc_in,
    cross_ref,
    near_ref,
    own_ref,
    token_ref,
    marks_ref,
):
    token_ref[...] = jnp.zeros_like(token_ref)
    fill_marks(marks_ref)
    lay = Layout(flip_here(tuned), q_ref, bias_ref, marks_ref)
    if tuned:
        head = lax.axis_index("head")
        beside = jnp.where((head == 0) | (head == lax.axis_size("head") - 1), 2, 3)
    else:
        beside = 2
    for row, keys, out in ((1, (2,), cross_ref), (beside, (2, 3), near_ref), (5 - beside, (2, 3), own_ref)):
        for side in range(2):
            pieces = [
                lay.piece(row, kr, side, far_ref.at[0], far_ref.at[1], flipped(kr - 2, lay.flip, 2)) for kr in keys
            ]
            at = pl.multiple_of((row - 1) * SPAN + side * HALF, HALF)
            before = [ref[pl.ds(at, HALF), :] for ref in (peak_in, total_in, acc_in)]
            out[side * HALF : (side + 1) * HALF, :] = finish(attend_block(lay.query(row, side), pieces, before))


def gate_kernel(*refs):
    pass


def stack_kernel(*refs):
    blocks, (out_ref, sems) = refs[:-3], refs[-2:]
    size = blocks[0].shape[0]
    copies = [
        pltpu.make_async_copy(block, out_ref.at[n * size : (n + 1) * size], sems.at[n]) for n, block in enumerate(blocks)
    ]
    for copy in start_all(copies):
        copy.wait()


def gate(blocks, name, flops=GATE_FLOPS):
    anywhere = pl.BlockSpec(memory_space=pl.ANY)
    return call(
        gate_kernel,
        name,
        [keep(block) for block in blocks],
        [pltpu.VMEM(block.shape, block.dtype) for block in blocks],
        [],
        [anywhere] * len(blocks),
        [anywhere] * len(blocks),
        [(n, n) for n in range(len(blocks))],
        flops,
    )


def call(kernel, name, ins, outs, scratch, specs=None, out_specs=None, aliases=(), flops=1_000_000):
    vmem = pl.BlockSpec(memory_space=pltpu.VMEM)
    return pl.pallas_call(
        kernel,
        out_shape=outs,
        in_specs=specs or [vmem] * len(ins),
        out_specs=tuple(out_specs or [vmem] * len(outs)),
        input_output_aliases=dict(aliases),
        scratch_shapes=scratch,
        compiler_params=pltpu.CompilerParams(vmem_limit_bytes=VMEM_BYTES),
        cost_estimate=pl.CostEstimate(flops=flops, bytes_accessed=1_000, transcendentals=0),
        name=name,
    )(*ins)


def assemble_kernel(shifts, own, *refs):
    stacks, whole = refs[:-1], refs[-1]
    frame, frames, head = lax.axis_index("frame"), lax.axis_size("frame"), lax.axis_index("head")
    y, core = frame // (frames // 2), frame % 2
    quarter = own.shape[0] // 4
    whole[head] = own[...]
    for n, stack in enumerate(stacks):
        row = (2 * (y ^ (n % 2)) + (core ^ (n // 2))) * quarter
        for m, shift in enumerate(shifts):
            whole[head ^ shift, pl.ds(pl.multiple_of(row, quarter), quarter), :] = stack[
                m * quarter : (m + 1) * quarter, :
            ]


def project_kernel(tuned, tile, *refs):
    parts, (weight_ref, out_hbm, out_ref, sems) = refs[:-4], refs[-4:]
    heads = weight_ref.shape[0]
    head = lax.axis_index("head")
    if tuned:
        own, near, early2, early3, late2, late3 = parts
        outer = (head == 0) | (head == heads - 1)
        blocks = [own[...], near[...], early2[...] + late2[...], early3[...] + late3[...]]
        first, second = jnp.where(outer, head ^ 2, head ^ 3), jnp.where(outer, head ^ 3, head ^ 2)
        order = [head, head ^ 1, first, second]
    else:
        blocks = [part[...] for part in parts]
        order = [head ^ s for s in range(heads)]
    rows = jnp.concatenate(blocks, axis=1)
    copies = []
    for n in range(weight_ref.shape[2] // tile):
        columns = slice(n * tile, (n + 1) * tile)
        weight = jnp.concatenate([weight_ref[h, :, columns] for h in order], axis=0)
        out_ref[:, columns] = jnp.dot(rows, weight, preferred_element_type=jnp.float32).astype(jnp.bfloat16)
        copies.append(pltpu.make_async_copy(out_ref.at[:, columns], out_hbm.at[:, columns], sems.at[n]))
        copies[-1].start()
    for copy in copies:
        copy.wait()


def project(tuned, parts, weight):
    tokens = parts[0].shape[0]
    heads, depth, width = weight.shape
    tile = 256
    vmem = pl.BlockSpec(memory_space=pltpu.VMEM)
    return pl.pallas_call(
        functools.partial(project_kernel, tuned, tile),
        out_shape=jax.ShapeDtypeStruct((tokens, width), jnp.bfloat16),
        in_specs=[vmem] * (len(parts) + 1),
        out_specs=pl.BlockSpec(memory_space=pltpu.HBM),
        scratch_shapes=[pltpu.VMEM((tokens, width), jnp.bfloat16), pltpu.SemaphoreType.DMA((width // tile,))],
        compiler_params=pltpu.CompilerParams(vmem_limit_bytes=VMEM_BYTES),
        name="project",
    )(*map(keep, parts), keep(weight))


def swap(block, axis, bit):
    return lax.ppermute(block, axis, [(i, i ^ bit) for i in range(lax.axis_size(axis))])


def on_device(queries, keys, values, block_mask, out_weight):
    frames = lax.axis_size("frame")
    heads = lax.axis_size("head")
    frame = lax.axis_index("frame")
    head = lax.axis_index("head")
    tuned = heads == TROWS
    mask = block_mask.reshape(TROWS * TCOLS, WIN)
    tokens = queries.shape[0]

    vmem, anywhere = pl.BlockSpec(memory_space=pltpu.VMEM), pl.BlockSpec(memory_space=pl.ANY)
    hbm = pl.BlockSpec(memory_space=pltpu.HBM)
    depth, width = out_weight.shape
    both = pltpu.VMEM((2, PAIR, HEAD_DIM), jnp.bfloat16)
    half0, half1, mine, query, mask = call(
        functools.partial(pack_kernel, tuned),
        "pack",
        (stay(keys), stay(values), stay(out_weight), stay(queries), stay(mask)),
        (
            both,
            both,
            pltpu.VMEM((depth // 4, width), out_weight.dtype),
            pltpu.VMEM(queries.shape, queries.dtype),
            pltpu.VMEM(mask.shape, mask.dtype),
        ),
        [pltpu.SemaphoreType.DMA((7,))],
        [hbm] * 5,
    )
    links = [(i, i + 1) for i in range(1, frames - 1, 2)]
    links += [(j, i) for i, j in links]
    far0 = lax.ppermute(half0, "frame", links)
    near = [swap(block, "frame", 1) for block in (half0, half1)]

    came = {s: swap(mine, "head", s) for s in ((3, 1) if tuned else range(1, heads))}

    marks = pltpu.VMEM((SPAN, 128), jnp.bfloat16)
    full = [pltpu.VMEM((tokens, 128), jnp.float32)] * 3
    three = [pltpu.VMEM((3 * SPAN, 128), jnp.float32)] * 3
    bias = pltpu.VMEM(BIAS_SHAPE, jnp.bfloat16)
    row = pltpu.VMEM((SPAN, HEAD_DIM), jnp.bfloat16)

    token = pltpu.VMEM((8, 128), jnp.float32)
    again, token_own, *state, bias_chip, bias_far = call(
        functools.partial(own_kernel, tuned),
        "attend_own",
        (keep(query), keep(mask), keep(half0), keep(half1)),
        (both, token, *full, bias, bias),
        [pltpu.VMEM((128, 128), jnp.float32), bias, marks, pltpu.SemaphoreType.DMA],
    )
    (far1,) = gate([lax.ppermute(again, "frame", links)], "gate_far")
    if tuned:
        came[3], came[1], _ = gate([came[3], came[1], token_own], "gate_own")
        came[2] = swap(came[3], "head", 1)
    *state, token_chip = call(
        functools.partial(chip_kernel, tuned),
        "attend_chip",
        (keep(query), *near, keep(bias_chip), *map(keep, state)),
        (*full, token),
        [marks],
    )
    shifts = sorted(came)
    (stacked,) = call(
        stack_kernel,
        "stack_weight",
        (*[keep(came[s]) for s in shifts], token_chip),
        [pltpu.VMEM((len(shifts) * depth // 4, width), out_weight.dtype)],
        [pltpu.SemaphoreType.DMA((len(shifts),))],
    )
    other = swap(stacked, "frame", frames // 2)
    first, *state = call(
        functools.partial(early_kernel, tuned),
        "attend_far_early",
        (keep(query), far0, keep(bias_far), *map(keep, state)),
        (row, *three),
        [marks],
    )
    cross, beside, own, token_late = call(
        functools.partial(late_kernel, tuned),
        "attend_far_late",
        (keep(query), keep(far1), keep(bias_far), *map(keep, state)),
        (row, row, row, token),
        [marks],
    )
    other, _ = gate([other, token_late], "gate_weight")
    stacks = [stacked, other, swap(stacked, "frame", 1), swap(other, "frame", 1)]
    (weight,) = call(
        functools.partial(assemble_kernel, tuple(shifts)),
        "assemble_weight",
        (out_weight, *map(keep, stacks)),
        (pltpu.VMEM((heads, depth, width), jnp.bfloat16),),
        [],
    )
    if tuned:
        early = [lax.ppermute(first, "head", [(3, 0), (0, 3)]), lax.ppermute(first, "head", [(2, 0), (1, 3)])]
        *early, _ = gate([*early, token_late], "gate_early")
        late = [lax.ppermute(cross, "head", [(3, 1), (0, 2)]), lax.ppermute(cross, "head", [(2, 1), (1, 2)])]
        parts = [swap(beside, "head", 1), early[1], early[0], late[1], late[0]]
        *parts, weight = gate([*parts, weight], "gate_late")
        parts = [own, *parts]
    else:
        rows = jnp.concatenate([first, cross, beside, own]).reshape(heads, tokens // heads, HEAD_DIM)
        parts = [lax.dynamic_index_in_dim(rows, head, 0, False)]
        for s in range(1, heads):
            parts.append(swap(lax.dynamic_index_in_dim(rows, head ^ s, 0, False), "head", s))
    return project(tuned, parts, weight)


def solution(mesh):
    return jax.shard_map(
        on_device,
        mesh=mesh,
        in_specs=(
            P("frame", "head"),
            P("frame", "head"),
            P("frame", "head"),
            P("head", "frame", None, None),
            P("head", None),
        ),
        out_specs=P(("frame", "head"), None),
        check_vma=False,
    )
```

```python
import functools
import math

import jax
import jax.numpy as jnp
from jax import lax
from jax.experimental import pallas as pl
from jax.experimental.pallas import tpu as pltpu
from jax.sharding import PartitionSpec as P

HEAD_DIM = 128
TROWS = 4
TCOLS = 8
WIN = 45
TILE = 64
SPAN = TCOLS * TILE
HALF = SPAN // 2
KEYS = 6 * TILE
SHIFT = 2 * TILE
PAIR = 2 * SPAN
FAR = -(2.0**100)
RATE = math.log2(math.e) / math.sqrt(HEAD_DIM)
BIAS_SHAPE = (TROWS * 3 * SPAN, 128)
VMEM_BYTES = 10 * 1024 * 1024
GATE_FLOPS = 20_000_000_000


def keep(block):
    return pltpu.with_memory_space_constraint(block, pltpu.VMEM)


def stay(block):
    return pltpu.with_memory_space_constraint(block, pltpu.HBM)


def fill_bias(mask_ref, padded_ref, frame, frames, bias_refs):
    padded_ref[...] = jnp.zeros_like(padded_ref)
    padded_ref[: TROWS * TCOLS, :WIN] = mask_ref[...].astype(jnp.float32)
    turned = padded_ref[...].T
    key_col = lax.broadcasted_iota(jnp.int32, (TCOLS, 128), 0)
    step = key_col - lax.broadcasted_iota(jnp.int32, (TCOLS, 128), 1)
    odd = frame % 2
    for r in range(TROWS):
        windows = turned if r == 0 else pltpu.roll(turned, 128 - r * TCOLS, 1)
        for b in range(3):
            if not 0 <= r + b - 1 < TROWS:
                continue
            picked = []
            for a in range(3):
                base = 15 * a + 5 * b + 2
                chosen = jnp.zeros((TCOLS, 128), jnp.float32)
                for d in range(-2, 3):
                    chosen = jnp.where(step == d, jnp.broadcast_to(windows[base + d : base + d + 1, :], (TCOLS, 128)), chosen)
                picked.append(chosen > 0)
            own = picked[1] | (step == 0) if b == 1 else picked[1]
            low = jnp.where(picked[0] & (frame > 0), 0.0, FAR)
            high = jnp.where(picked[2] & (frame < frames - 1), 0.0, FAR)
            for ref, bias in zip(
                bias_refs,
                (jnp.where(own, 0.0, FAR), jnp.where(odd == 1, low, high), jnp.where(odd == 1, high, low)),
            ):
                for k in range(TCOLS):
                    start = (r * 3 + b) * SPAN + k * TILE
                    ref[start : start + TILE, :] = jnp.broadcast_to(bias[k : k + 1, :], (TILE, 128)).astype(
                        jnp.bfloat16
                    )


def fill_marks(marks_ref):
    tile = lax.broadcasted_iota(jnp.int32, (SPAN, 128), 0) // TILE
    lane = lax.broadcasted_iota(jnp.int32, (SPAN, 128), 1)
    marks_ref[...] = (lane == tile).astype(jnp.float32).astype(jnp.bfloat16)


def attend_block(query, pieces, before):
    keys = jnp.concatenate([jnp.concatenate([key, bias], axis=1) for key, bias, _ in pieces], axis=0)
    values = jnp.concatenate([value for _, _, value in pieces], axis=0)
    values = jnp.concatenate([values, jnp.ones_like(values)], axis=1)
    scores = lax.dot_general(query, keys, (((1,), (1,)), ((), ())), preferred_element_type=jnp.float32)
    peak = jnp.max(scores, axis=1, keepdims=True)
    if before is not None:
        peak = jnp.maximum(peak, before[0][:, :1])
    expo = jnp.exp2((scores - peak) * RATE).astype(jnp.bfloat16)
    acc = jnp.dot(expo, values, preferred_element_type=jnp.float32)
    total, acc = acc[:, HEAD_DIM:], acc[:, :HEAD_DIM]
    if before is not None:
        fade = jnp.exp2((before[0] - peak) * RATE)
        total = total + fade * before[1]
        acc = acc + fade * before[2]
    return peak, total, acc


def flipped(row, flip, rows):
    return row + flip * (rows - 1 - 2 * row)


class Layout:
    def __init__(self, flip, q_ref, bias_ref, marks_ref):
        self.flip, self.q, self.bias, self.marks = flip, q_ref, bias_ref, marks_ref

    def query(self, row, side):
        at = pl.multiple_of(flipped(row, self.flip, TROWS) * SPAN + side * HALF, HALF)
        return jnp.concatenate([self.q[pl.ds(at, HALF), :], self.marks[side * HALF : (side + 1) * HALF, :]], axis=1)

    def piece(self, row, key_row, side, k_ref, v_ref, at_row):
        r, kr = flipped(row, self.flip, TROWS), flipped(key_row, self.flip, TROWS)
        at = pl.multiple_of((r * 3 + kr - r + 1) * SPAN + side * SHIFT, SHIFT)
        start = pl.multiple_of(at_row * SPAN + side * SHIFT, SHIFT)
        return (
            k_ref[pl.ds(start, KEYS), :],
            self.bias[pl.ds(at, KEYS), :],
            v_ref[pl.ds(start, KEYS), :],
        )


    def both(self, row, side, half0, half1):
        pieces = []
        for kr in around(row):
            half = (half0, half1)[kr // 2]
            pieces.append(self.piece(row, kr, side, half.at[0], half.at[1], flipped(kr % 2, self.flip, 2)))
        return pieces


def around(row):
    return range(max(row - 1, 0), min(row + 1, TROWS - 1) + 1)


def put(refs, at, state):
    for ref, value in zip(refs, state):
        ref[at : at + HALF, :] = jnp.broadcast_to(value, (HALF, 128))


def get(refs, at):
    return [ref[at : at + HALF, :] for ref in refs]


def flip_here(tuned):
    return (lax.axis_index("head") < lax.axis_size("head") // 2).astype(jnp.int32) if tuned else jnp.int32(0)


def start_all(copies):
    for copy in copies:
        copy.start()
    return copies


def pack_kernel(tuned, k_ref, v_ref, weight_ref, q_hbm, mask_hbm, first_ref, second_ref, mine_ref, q_ref, mask_ref, sems):
    flip = flip_here(tuned)
    half = mine_ref.shape[0]
    frame = lax.axis_index("frame")
    row = pl.multiple_of(frame % 2 * half, half)
    moves = []
    for i, out in enumerate((first_ref, second_ref)):
        start = pl.multiple_of((flip if i == 0 else 1 - flip) * PAIR, PAIR)
        moves += [(source.at[pl.ds(start, PAIR)], out.at[j]) for j, source in enumerate((k_ref, v_ref))]
    moves += [(weight_ref.at[pl.ds(row, half)], mine_ref), (q_hbm, q_ref), (mask_hbm, mask_ref)]
    for copy in start_all([pltpu.make_async_copy(a, b, sems.at[n]) for n, (a, b) in enumerate(moves)]):
        copy.wait()


def own_kernel(
    tuned,
    q_ref,
    mask_ref,
    half0,
    half1,
    again_ref,
    token_ref,
    peak,
    total,
    acc,
    bias_chip,
    bias_far,
    padded_ref,
    bias_ref,
    marks_ref,
    sem,
):
    token_ref[...] = jnp.zeros_like(token_ref)
    copy = pltpu.make_async_copy(half1, again_ref, sem)
    copy.start()
    fill_marks(marks_ref)
    fill_bias(
        mask_ref, padded_ref, lax.axis_index("frame"), lax.axis_size("frame"), (bias_ref, bias_chip, bias_far)
    )
    lay = Layout(flip_here(tuned), q_ref, bias_ref, marks_ref)
    for row in range(TROWS):
        for side in range(2):
            pieces = lay.both(row, side, half0, half1)
            put((peak, total, acc), row * SPAN + side * HALF, attend_block(lay.query(row, side), pieces, None))
    copy.wait()


def chip_kernel(
    tuned, q_ref, near0, near1, bias_ref, peak_in, total_in, acc_in, peak, total, acc, token_ref, marks_ref
):
    token_ref[...] = jnp.zeros_like(token_ref)
    fill_marks(marks_ref)
    lay = Layout(flip_here(tuned), q_ref, bias_ref, marks_ref)
    for row in range(TROWS):
        for side in range(2):
            at = row * SPAN + side * HALF
            before = get((peak_in, total_in, acc_in), at)
            state = attend_block(lay.query(row, side), lay.both(row, side, near0, near1), before)
            put((peak, total, acc), at, state)


def finish(state):
    return (state[2] / state[1]).astype(jnp.bfloat16)


def early_kernel(
    tuned, q_ref, far0, bias_ref, peak_in, total_in, acc_in, out_ref, peak, total, acc, token_ref, marks_ref
):
    token_ref[...] = jnp.zeros_like(token_ref)
    fill_marks(marks_ref)
    for new, old in zip((peak, total, acc), (peak_in, total_in, acc_in)):
        new[PAIR:, :] = old[3 * SPAN :, :]
    lay = Layout(flip_here(tuned), q_ref, bias_ref, marks_ref)
    for row in range(3):
        for side in range(2):
            pieces = [
                lay.piece(row, kr, side, far0.at[0], far0.at[1], flipped(kr, lay.flip, 2))
                for kr in around(row)
                if kr < 2
            ]
            at = row * SPAN + side * HALF
            state = attend_block(lay.query(row, side), pieces, get((peak_in, total_in, acc_in), at))
            if row == 0:
                out_ref[side * HALF : (side + 1) * HALF, :] = finish(state)
            else:
                put((peak, total, acc), at - SPAN, state)


def late_kernel(
    tuned,
    q_ref,
    far_ref,
    bias_ref,
    peak_in,
    total_in,
    acc_in,
    cross_ref,
    near_ref,
    own_ref,
    token_ref,
    marks_ref,
):
    token_ref[...] = jnp.zeros_like(token_ref)
    fill_marks(marks_ref)
    lay = Layout(flip_here(tuned), q_ref, bias_ref, marks_ref)
    if tuned:
        head = lax.axis_index("head")
        beside = jnp.where((head == 0) | (head == lax.axis_size("head") - 1), 2, 3)
    else:
        beside = 2
    for row, keys, out in ((1, (2,), cross_ref), (beside, (2, 3), near_ref), (5 - beside, (2, 3), own_ref)):
        for side in range(2):
            pieces = [
                lay.piece(row, kr, side, far_ref.at[0], far_ref.at[1], flipped(kr - 2, lay.flip, 2)) for kr in keys
            ]
            at = pl.multiple_of((row - 1) * SPAN + side * HALF, HALF)
            before = [ref[pl.ds(at, HALF), :] for ref in (peak_in, total_in, acc_in)]
            out[side * HALF : (side + 1) * HALF, :] = finish(attend_block(lay.query(row, side), pieces, before))


def gate_kernel(*refs):
    pass


def gate(blocks, name, flops=GATE_FLOPS):
    anywhere = pl.BlockSpec(memory_space=pl.ANY)
    return call(
        gate_kernel,
        name,
        [keep(block) for block in blocks],
        [pltpu.VMEM(block.shape, block.dtype) for block in blocks],
        [],
        [anywhere] * len(blocks),
        [anywhere] * len(blocks),
        [(n, n) for n in range(len(blocks))],
        flops,
    )


def call(kernel, name, ins, outs, scratch, specs=None, out_specs=None, aliases=(), flops=1_000_000):
    vmem = pl.BlockSpec(memory_space=pltpu.VMEM)
    return pl.pallas_call(
        kernel,
        out_shape=outs,
        in_specs=specs or [vmem] * len(ins),
        out_specs=tuple(out_specs or [vmem] * len(outs)),
        input_output_aliases=dict(aliases),
        scratch_shapes=scratch,
        compiler_params=pltpu.CompilerParams(vmem_limit_bytes=VMEM_BYTES),
        cost_estimate=pl.CostEstimate(flops=flops, bytes_accessed=1_000, transcendentals=0),
        name=name,
    )(*ins)


def assemble_kernel(shifts, own, *refs):
    pieces, whole = refs[:-1], refs[-1]
    core, head = lax.axis_index("frame") % 2, lax.axis_index("head")
    half = own.shape[0] // 2
    whole[head] = own[...]
    for n, piece in enumerate(pieces):
        row = (core if n % 2 == 0 else 1 - core) * half
        whole[head ^ shifts[n // 2], pl.ds(pl.multiple_of(row, half), half), :] = piece[...]


def project_kernel(tuned, tile, *refs):
    parts, (weight_ref, out_hbm, out_ref, sems) = refs[:-4], refs[-4:]
    heads = weight_ref.shape[0]
    head = lax.axis_index("head")
    if tuned:
        own, near, early2, early3, late2, late3 = parts
        outer = (head == 0) | (head == heads - 1)
        blocks = [own[...], near[...], early2[...] + late2[...], early3[...] + late3[...]]
        first, second = jnp.where(outer, head ^ 2, head ^ 3), jnp.where(outer, head ^ 3, head ^ 2)
        order = [head, head ^ 1, first, second]
    else:
        blocks = [part[...] for part in parts]
        order = [head ^ s for s in range(heads)]
    rows = jnp.concatenate(blocks, axis=1)
    copies = []
    for n in range(weight_ref.shape[2] // tile):
        columns = slice(n * tile, (n + 1) * tile)
        weight = jnp.concatenate([weight_ref[h, :, columns] for h in order], axis=0)
        out_ref[:, columns] = jnp.dot(rows, weight, preferred_element_type=jnp.float32).astype(jnp.bfloat16)
        copies.append(pltpu.make_async_copy(out_ref.at[:, columns], out_hbm.at[:, columns], sems.at[n]))
        copies[-1].start()
    for copy in copies:
        copy.wait()


def project(tuned, parts, weight):
    tokens = parts[0].shape[0]
    heads, depth, width = weight.shape
    tile = 256
    vmem = pl.BlockSpec(memory_space=pltpu.VMEM)
    return pl.pallas_call(
        functools.partial(project_kernel, tuned, tile),
        out_shape=jax.ShapeDtypeStruct((tokens, width), jnp.bfloat16),
        in_specs=[vmem] * (len(parts) + 1),
        out_specs=pl.BlockSpec(memory_space=pltpu.HBM),
        scratch_shapes=[pltpu.VMEM((tokens, width), jnp.bfloat16), pltpu.SemaphoreType.DMA((width // tile,))],
        compiler_params=pltpu.CompilerParams(vmem_limit_bytes=VMEM_BYTES),
        name="project",
    )(*map(keep, parts), keep(weight))


def swap(block, axis, bit):
    return lax.ppermute(block, axis, [(i, i ^ bit) for i in range(lax.axis_size(axis))])


def on_device(queries, keys, values, block_mask, out_weight):
    frames = lax.axis_size("frame")
    heads = lax.axis_size("head")
    frame = lax.axis_index("frame")
    head = lax.axis_index("head")
    tuned = heads == TROWS
    mask = block_mask.reshape(TROWS * TCOLS, WIN)
    tokens = queries.shape[0]

    vmem, anywhere = pl.BlockSpec(memory_space=pltpu.VMEM), pl.BlockSpec(memory_space=pl.ANY)
    hbm = pl.BlockSpec(memory_space=pltpu.HBM)
    depth, width = out_weight.shape
    both = pltpu.VMEM((2, PAIR, HEAD_DIM), jnp.bfloat16)
    half0, half1, mine, query, mask = call(
        functools.partial(pack_kernel, tuned),
        "pack",
        (stay(keys), stay(values), stay(out_weight), stay(queries), stay(mask)),
        (
            both,
            both,
            pltpu.VMEM((depth // 2, width), out_weight.dtype),
            pltpu.VMEM(queries.shape, queries.dtype),
            pltpu.VMEM(mask.shape, mask.dtype),
        ),
        [pltpu.SemaphoreType.DMA((7,))],
        [hbm] * 5,
    )
    links = [(i, i + 1) for i in range(1, frames - 1, 2)]
    links += [(j, i) for i, j in links]
    far0 = lax.ppermute(half0, "frame", links)
    near = [swap(block, "frame", 1) for block in (half0, half1)]

    came = {s: swap(mine, "head", s) for s in ((3, 1) if tuned else range(1, heads))}

    marks = pltpu.VMEM((SPAN, 128), jnp.bfloat16)
    full = [pltpu.VMEM((tokens, 128), jnp.float32)] * 3
    three = [pltpu.VMEM((3 * SPAN, 128), jnp.float32)] * 3
    bias = pltpu.VMEM(BIAS_SHAPE, jnp.bfloat16)
    row = pltpu.VMEM((SPAN, HEAD_DIM), jnp.bfloat16)

    token = pltpu.VMEM((8, 128), jnp.float32)
    again, token_own, *state, bias_chip, bias_far = call(
        functools.partial(own_kernel, tuned),
        "attend_own",
        (keep(query), keep(mask), keep(half0), keep(half1)),
        (both, token, *full, bias, bias),
        [pltpu.VMEM((128, 128), jnp.float32), bias, marks, pltpu.SemaphoreType.DMA],
    )
    (far1,) = gate([lax.ppermute(again, "frame", links)], "gate_far")
    *state, token_chip = call(
        functools.partial(chip_kernel, tuned),
        "attend_chip",
        (keep(query), *near, keep(bias_chip), *map(keep, state)),
        (*full, token),
        [marks],
    )
    first, *state, token_early = call(
        functools.partial(early_kernel, tuned),
        "attend_far_early",
        (keep(query), far0, keep(bias_far), *map(keep, state)),
        (row, *three, token),
        [marks],
    )
    if tuned:
        came[3], came[1], _ = gate([came[3], came[1], token_early], "gate_came")
        came[2] = swap(came[3], "head", 1)
    cross, beside, own, token_late = call(
        functools.partial(late_kernel, tuned),
        "attend_far_late",
        (keep(query), keep(far1), keep(bias_far), *map(keep, state)),
        (row, row, row, token),
        [marks],
    )
    if tuned:
        early = [lax.ppermute(first, "head", [(2, 0), (1, 3)]), lax.ppermute(first, "head", [(3, 0), (0, 3)])]
        late = [lax.ppermute(cross, "head", [(3, 1), (0, 2)]), lax.ppermute(cross, "head", [(2, 1), (1, 2)])]
        late += [swap(beside, "head", 1)]
        came[2], *early, _ = gate([came[2], *early, token_late], "gate_early")
    shifts = [1, 3, 2] if tuned else list(came)
    pieces = [piece for s in shifts for piece in (came[s], swap(came[s], "frame", 1))]
    (weight,) = call(
        functools.partial(assemble_kernel, tuple(shifts)),
        "assemble_weight",
        (out_weight, *map(keep, pieces)),
        (pltpu.VMEM((heads, depth, width), jnp.bfloat16),),
        [],
    )
    if tuned:
        late = gate(late, "gate_late")
        *early, late3, late2, beside, weight = gate([*early, *late, weight], "gate_all")
        parts = [own, beside, *early, late2, late3]
    else:
        rows = jnp.concatenate([first, cross, beside, own]).reshape(heads, tokens // heads, HEAD_DIM)
        parts = [lax.dynamic_index_in_dim(rows, head, 0, False)]
        for s in range(1, heads):
            parts.append(swap(lax.dynamic_index_in_dim(rows, head ^ s, 0, False), "head", s))
    return project(tuned, parts, weight)


def solution(mesh):
    return jax.shard_map(
        on_device,
        mesh=mesh,
        in_specs=(
            P("frame", "head"),
            P("frame", "head"),
            P("frame", "head"),
            P("head", "frame", None, None),
            P("head", None),
        ),
        out_specs=P(("frame", "head"), None),
        check_vma=False,
    )
```

```python
import functools
import math

import jax
import jax.numpy as jnp
from jax import lax
from jax.experimental import pallas as pl
from jax.experimental.pallas import tpu as pltpu
from jax.sharding import PartitionSpec as P

HEAD_DIM = 128
TROWS = 4
TCOLS = 8
WIN = 45
TILE = 64
SPAN = TCOLS * TILE
HALF = SPAN // 2
KEYS = 6 * TILE
SHIFT = 2 * TILE
PAIR = 2 * SPAN
FAR = -(2.0**100)
RATE = math.log2(math.e) / math.sqrt(HEAD_DIM)
BIAS_SHAPE = (TROWS * 3 * SPAN, 128)
VMEM_BYTES = 10 * 1024 * 1024
GATE_FLOPS = 20_000_000_000


def keep(block):
    return pltpu.with_memory_space_constraint(block, pltpu.VMEM)


def stay(block):
    return pltpu.with_memory_space_constraint(block, pltpu.HBM)


def fill_bias(mask_ref, padded_ref, frame, frames, bias_refs):
    padded_ref[...] = jnp.zeros_like(padded_ref)
    padded_ref[: TROWS * TCOLS, :WIN] = mask_ref[...].astype(jnp.float32)
    turned = padded_ref[...].T
    key_col = lax.broadcasted_iota(jnp.int32, (TCOLS, 128), 0)
    step = key_col - lax.broadcasted_iota(jnp.int32, (TCOLS, 128), 1)
    odd = frame % 2
    for r in range(TROWS):
        windows = turned if r == 0 else pltpu.roll(turned, 128 - r * TCOLS, 1)
        for b in range(3):
            if not 0 <= r + b - 1 < TROWS:
                continue
            picked = []
            for a in range(3):
                base = 15 * a + 5 * b + 2
                chosen = jnp.zeros((TCOLS, 128), jnp.float32)
                for d in range(-2, 3):
                    chosen = jnp.where(step == d, jnp.broadcast_to(windows[base + d : base + d + 1, :], (TCOLS, 128)), chosen)
                picked.append(chosen > 0)
            own = picked[1] | (step == 0) if b == 1 else picked[1]
            low = jnp.where(picked[0] & (frame > 0), 0.0, FAR)
            high = jnp.where(picked[2] & (frame < frames - 1), 0.0, FAR)
            for ref, bias in zip(
                bias_refs,
                (jnp.where(own, 0.0, FAR), jnp.where(odd == 1, low, high), jnp.where(odd == 1, high, low)),
            ):
                for k in range(TCOLS):
                    start = (r * 3 + b) * SPAN + k * TILE
                    ref[start : start + TILE, :] = jnp.broadcast_to(bias[k : k + 1, :], (TILE, 128)).astype(
                        jnp.bfloat16
                    )


def fill_marks(marks_ref):
    tile = lax.broadcasted_iota(jnp.int32, (SPAN, 128), 0) // TILE
    lane = lax.broadcasted_iota(jnp.int32, (SPAN, 128), 1)
    marks_ref[...] = (lane == tile).astype(jnp.float32).astype(jnp.bfloat16)


def attend_block(query, pieces, before):
    keys = jnp.concatenate([jnp.concatenate([key, bias], axis=1) for key, bias, _ in pieces], axis=0)
    values = jnp.concatenate([value for _, _, value in pieces], axis=0)
    values = jnp.concatenate([values, jnp.ones_like(values)], axis=1)
    scores = lax.dot_general(query, keys, (((1,), (1,)), ((), ())), preferred_element_type=jnp.float32)
    peak = jnp.max(scores, axis=1, keepdims=True)
    if before is not None:
        peak = jnp.maximum(peak, before[0][:, :1])
    expo = jnp.exp2((scores - peak) * RATE).astype(jnp.bfloat16)
    acc = jnp.dot(expo, values, preferred_element_type=jnp.float32)
    total, acc = acc[:, HEAD_DIM:], acc[:, :HEAD_DIM]
    if before is not None:
        fade = jnp.exp2((before[0] - peak) * RATE)
        total = total + fade * before[1]
        acc = acc + fade * before[2]
    return peak, total, acc


def flipped(row, flip, rows):
    return row + flip * (rows - 1 - 2 * row)


class Layout:
    def __init__(self, flip, q_ref, bias_ref, marks_ref):
        self.flip, self.q, self.bias, self.marks = flip, q_ref, bias_ref, marks_ref

    def query(self, row, side):
        at = pl.multiple_of(flipped(row, self.flip, TROWS) * SPAN + side * HALF, HALF)
        return jnp.concatenate([self.q[pl.ds(at, HALF), :], self.marks[side * HALF : (side + 1) * HALF, :]], axis=1)

    def piece(self, row, key_row, side, k_ref, v_ref, at_row):
        r, kr = flipped(row, self.flip, TROWS), flipped(key_row, self.flip, TROWS)
        at = pl.multiple_of((r * 3 + kr - r + 1) * SPAN + side * SHIFT, SHIFT)
        start = pl.multiple_of(at_row * SPAN + side * SHIFT, SHIFT)
        return (
            k_ref[pl.ds(start, KEYS), :],
            self.bias[pl.ds(at, KEYS), :],
            v_ref[pl.ds(start, KEYS), :],
        )


    def both(self, row, side, half0, half1):
        pieces = []
        for kr in around(row):
            half = (half0, half1)[kr // 2]
            pieces.append(self.piece(row, kr, side, half.at[0], half.at[1], flipped(kr % 2, self.flip, 2)))
        return pieces


def around(row):
    return range(max(row - 1, 0), min(row + 1, TROWS - 1) + 1)


def put(refs, at, state):
    for ref, value in zip(refs, state):
        ref[at : at + HALF, :] = jnp.broadcast_to(value, (HALF, 128))


def get(refs, at):
    return [ref[at : at + HALF, :] for ref in refs]


def flip_here(tuned):
    return (lax.axis_index("head") < lax.axis_size("head") // 2).astype(jnp.int32) if tuned else jnp.int32(0)


def start_all(copies):
    for copy in copies:
        copy.start()
    return copies


def pack_kernel(
    tuned, k_ref, v_ref, weight_ref, q_hbm, mask_hbm, first_ref, second_ref, mine_ref, less_ref, q_ref, mask_ref, sems
):
    flip = flip_here(tuned)
    half = mine_ref.shape[0]
    frame = lax.axis_index("frame")
    row = pl.multiple_of(frame % 2 * half, half)
    quarter = less_ref.shape[0]
    part = pl.multiple_of(row + frame // (lax.axis_size("frame") // 2) * quarter, quarter)
    moves = []
    for i, out in enumerate((first_ref, second_ref)):
        start = pl.multiple_of((flip if i == 0 else 1 - flip) * PAIR, PAIR)
        moves += [(source.at[pl.ds(start, PAIR)], out.at[j]) for j, source in enumerate((k_ref, v_ref))]
    moves += [(weight_ref.at[pl.ds(row, half)], mine_ref), (weight_ref.at[pl.ds(part, quarter)], less_ref), (q_hbm, q_ref), (mask_hbm, mask_ref)]
    for copy in start_all([pltpu.make_async_copy(a, b, sems.at[n]) for n, (a, b) in enumerate(moves)]):
        copy.wait()


def own_kernel(
    tuned,
    q_ref,
    mask_ref,
    half0,
    half1,
    again_ref,
    token_ref,
    peak,
    total,
    acc,
    bias_chip,
    bias_far,
    padded_ref,
    bias_ref,
    marks_ref,
    sem,
):
    token_ref[...] = jnp.zeros_like(token_ref)
    copy = pltpu.make_async_copy(half1, again_ref, sem)
    copy.start()
    fill_marks(marks_ref)
    fill_bias(
        mask_ref, padded_ref, lax.axis_index("frame"), lax.axis_size("frame"), (bias_ref, bias_chip, bias_far)
    )
    lay = Layout(flip_here(tuned), q_ref, bias_ref, marks_ref)
    for row in range(TROWS):
        for side in range(2):
            pieces = lay.both(row, side, half0, half1)
            put((peak, total, acc), row * SPAN + side * HALF, attend_block(lay.query(row, side), pieces, None))
    copy.wait()


def chip_kernel(
    tuned, q_ref, near0, near1, bias_ref, peak_in, total_in, acc_in, peak, total, acc, token_ref, marks_ref
):
    token_ref[...] = jnp.zeros_like(token_ref)
    fill_marks(marks_ref)
    lay = Layout(flip_here(tuned), q_ref, bias_ref, marks_ref)
    for row in range(TROWS):
        for side in range(2):
            at = row * SPAN + side * HALF
            before = get((peak_in, total_in, acc_in), at)
            state = attend_block(lay.query(row, side), lay.both(row, side, near0, near1), before)
            put((peak, total, acc), at, state)


def finish(state):
    return (state[2] / state[1]).astype(jnp.bfloat16)


def early_kernel(
    tuned, q_ref, far0, bias_ref, peak_in, total_in, acc_in, out_ref, peak, total, acc, token_ref, marks_ref
):
    token_ref[...] = jnp.zeros_like(token_ref)
    fill_marks(marks_ref)
    for new, old in zip((peak, total, acc), (peak_in, total_in, acc_in)):
        new[PAIR:, :] = old[3 * SPAN :, :]
    lay = Layout(flip_here(tuned), q_ref, bias_ref, marks_ref)
    for row in range(3):
        for side in range(2):
            pieces = [
                lay.piece(row, kr, side, far0.at[0], far0.at[1], flipped(kr, lay.flip, 2))
                for kr in around(row)
                if kr < 2
            ]
            at = row * SPAN + side * HALF
            state = attend_block(lay.query(row, side), pieces, get((peak_in, total_in, acc_in), at))
            if row == 0:
                out_ref[side * HALF : (side + 1) * HALF, :] = finish(state)
            else:
                put((peak, total, acc), at - SPAN, state)


def late_kernel(
    tuned,
    q_ref,
    far_ref,
    bias_ref,
    peak_in,
    total_in,
    acc_in,
    cross_ref,
    near_ref,
    own_ref,
    token_ref,
    marks_ref,
):
    token_ref[...] = jnp.zeros_like(token_ref)
    fill_marks(marks_ref)
    lay = Layout(flip_here(tuned), q_ref, bias_ref, marks_ref)
    if tuned:
        head = lax.axis_index("head")
        beside = jnp.where((head == 0) | (head == lax.axis_size("head") - 1), 2, 3)
    else:
        beside = 2
    for row, keys, out in ((1, (2,), cross_ref), (beside, (2, 3), near_ref), (5 - beside, (2, 3), own_ref)):
        for side in range(2):
            pieces = [
                lay.piece(row, kr, side, far_ref.at[0], far_ref.at[1], flipped(kr - 2, lay.flip, 2)) for kr in keys
            ]
            at = pl.multiple_of((row - 1) * SPAN + side * HALF, HALF)
            before = [ref[pl.ds(at, HALF), :] for ref in (peak_in, total_in, acc_in)]
            out[side * HALF : (side + 1) * HALF, :] = finish(attend_block(lay.query(row, side), pieces, before))


def gate_kernel(*refs):
    pass


def stack_kernel(*refs):
    blocks, (out_ref, sems) = refs[:-3], refs[-2:]
    size = blocks[0].shape[0]
    copies = [
        pltpu.make_async_copy(block, out_ref.at[n * size : (n + 1) * size], sems.at[n]) for n, block in enumerate(blocks)
    ]
    for copy in start_all(copies):
        copy.wait()


def gate(blocks, name, flops=GATE_FLOPS):
    anywhere = pl.BlockSpec(memory_space=pl.ANY)
    return call(
        gate_kernel,
        name,
        [keep(block) for block in blocks],
        [pltpu.VMEM(block.shape, block.dtype) for block in blocks],
        [],
        [anywhere] * len(blocks),
        [anywhere] * len(blocks),
        [(n, n) for n in range(len(blocks))],
        flops,
    )


def call(kernel, name, ins, outs, scratch, specs=None, out_specs=None, aliases=(), flops=1_000_000):
    vmem = pl.BlockSpec(memory_space=pltpu.VMEM)
    return pl.pallas_call(
        kernel,
        out_shape=outs,
        in_specs=specs or [vmem] * len(ins),
        out_specs=tuple(out_specs or [vmem] * len(outs)),
        input_output_aliases=dict(aliases),
        scratch_shapes=scratch,
        compiler_params=pltpu.CompilerParams(vmem_limit_bytes=VMEM_BYTES),
        cost_estimate=pl.CostEstimate(flops=flops, bytes_accessed=1_000, transcendentals=0),
        name=name,
    )(*ins)


def assemble_kernel(tuned, shifts, own, *refs):
    pieces, whole = refs[:-1], refs[-1]
    frame, head = lax.axis_index("frame"), lax.axis_index("head")
    core = frame % 2
    half = own.shape[0] // 2
    whole[head] = own[...]

    def place(shift, row, piece):
        size = piece.shape[0]
        whole[head ^ shift, pl.ds(pl.multiple_of(row, size), size), :] = piece[...]

    for n, piece in enumerate(pieces[:2] if tuned else pieces):
        place(shifts[n // 2], (core if n % 2 == 0 else 1 - core) * half, piece)
    if tuned:
        quarter = half // 2
        y = frame // (lax.axis_size("frame") // 2)
        for n, piece in enumerate(pieces[2:]):
            row = (core ^ (n // 2)) * half + (y ^ (n % 2)) * quarter
            for m, shift in enumerate(shifts[1:]):
                place(shift, row, piece.at[m * quarter : (m + 1) * quarter])


def project_kernel(tuned, tile, *refs):
    parts, (weight_ref, out_hbm, out_ref, sems) = refs[:-4], refs[-4:]
    heads = weight_ref.shape[0]
    head = lax.axis_index("head")
    if tuned:
        own, near, early2, early3, late2, late3 = parts
        outer = (head == 0) | (head == heads - 1)
        blocks = [own[...], near[...], early2[...] + late2[...], early3[...] + late3[...]]
        first, second = jnp.where(outer, head ^ 2, head ^ 3), jnp.where(outer, head ^ 3, head ^ 2)
        order = [head, head ^ 1, first, second]
    else:
        blocks = [part[...] for part in parts]
        order = [head ^ s for s in range(heads)]
    rows = jnp.concatenate(blocks, axis=1)
    copies = []
    for n in range(weight_ref.shape[2] // tile):
        columns = slice(n * tile, (n + 1) * tile)
        weight = jnp.concatenate([weight_ref[h, :, columns] for h in order], axis=0)
        out_ref[:, columns] = jnp.dot(rows, weight, preferred_element_type=jnp.float32).astype(jnp.bfloat16)
        copies.append(pltpu.make_async_copy(out_ref.at[:, columns], out_hbm.at[:, columns], sems.at[n]))
        copies[-1].start()
    for copy in copies:
        copy.wait()


def project(tuned, parts, weight):
    tokens = parts[0].shape[0]
    heads, depth, width = weight.shape
    tile = 256
    vmem = pl.BlockSpec(memory_space=pltpu.VMEM)
    return pl.pallas_call(
        functools.partial(project_kernel, tuned, tile),
        out_shape=jax.ShapeDtypeStruct((tokens, width), jnp.bfloat16),
        in_specs=[vmem] * (len(parts) + 1),
        out_specs=pl.BlockSpec(memory_space=pltpu.HBM),
        scratch_shapes=[pltpu.VMEM((tokens, width), jnp.bfloat16), pltpu.SemaphoreType.DMA((width // tile,))],
        compiler_params=pltpu.CompilerParams(vmem_limit_bytes=VMEM_BYTES),
        name="project",
    )(*map(keep, parts), keep(weight))


def swap(block, axis, bit):
    return lax.ppermute(block, axis, [(i, i ^ bit) for i in range(lax.axis_size(axis))])


def on_device(queries, keys, values, block_mask, out_weight):
    frames = lax.axis_size("frame")
    heads = lax.axis_size("head")
    frame = lax.axis_index("frame")
    head = lax.axis_index("head")
    tuned = heads == TROWS
    mask = block_mask.reshape(TROWS * TCOLS, WIN)
    tokens = queries.shape[0]

    vmem, anywhere = pl.BlockSpec(memory_space=pltpu.VMEM), pl.BlockSpec(memory_space=pl.ANY)
    hbm = pl.BlockSpec(memory_space=pltpu.HBM)
    depth, width = out_weight.shape
    both = pltpu.VMEM((2, PAIR, HEAD_DIM), jnp.bfloat16)
    half0, half1, mine, less, query, mask = call(
        functools.partial(pack_kernel, tuned),
        "pack",
        (stay(keys), stay(values), stay(out_weight), stay(queries), stay(mask)),
        (
            both,
            both,
            pltpu.VMEM((depth // 2, width), out_weight.dtype),
            pltpu.VMEM((depth // 4, width), out_weight.dtype),
            pltpu.VMEM(queries.shape, queries.dtype),
            pltpu.VMEM(mask.shape, mask.dtype),
        ),
        [pltpu.SemaphoreType.DMA((8,))],
        [hbm] * 5,
    )
    links = [(i, i + 1) for i in range(1, frames - 1, 2)]
    links += [(j, i) for i, j in links]
    far0 = lax.ppermute(half0, "frame", links)
    near = [swap(block, "frame", 1) for block in (half0, half1)]

    if tuned:
        came = {3: swap(less, "head", 3), 1: swap(mine, "head", 1)}
    else:
        came = {s: swap(mine, "head", s) for s in range(1, heads)}

    marks = pltpu.VMEM((SPAN, 128), jnp.bfloat16)
    full = [pltpu.VMEM((tokens, 128), jnp.float32)] * 3
    three = [pltpu.VMEM((3 * SPAN, 128), jnp.float32)] * 3
    bias = pltpu.VMEM(BIAS_SHAPE, jnp.bfloat16)
    row = pltpu.VMEM((SPAN, HEAD_DIM), jnp.bfloat16)

    token = pltpu.VMEM((8, 128), jnp.float32)
    again, token_own, *state, bias_chip, bias_far = call(
        functools.partial(own_kernel, tuned),
        "attend_own",
        (keep(query), keep(mask), keep(half0), keep(half1)),
        (both, token, *full, bias, bias),
        [pltpu.VMEM((128, 128), jnp.float32), bias, marks, pltpu.SemaphoreType.DMA],
    )
    (far1,) = gate([lax.ppermute(again, "frame", links)], "gate_far")
    if tuned:
        came[3], _ = gate([came[3], token_own], "gate_own")
        came[2] = swap(came[3], "head", 1)
    *state, token_chip = call(
        functools.partial(chip_kernel, tuned),
        "attend_chip",
        (keep(query), *near, keep(bias_chip), *map(keep, state)),
        (*full, token),
        [marks],
    )
    if tuned:
        came[1], token_chip = gate([came[1], token_chip], "gate_middle")
        far0, _ = gate([far0, token_chip], "gate_halo")
    first, *state, token_early = call(
        functools.partial(early_kernel, tuned),
        "attend_far_early",
        (keep(query), far0, keep(bias_far), *map(keep, state)),
        (row, *three, token),
        [marks],
    )
    if tuned:
        (stacked,) = call(
            stack_kernel,
            "stack_weight",
            (keep(came[3]), keep(came[2]), token_early),
            [pltpu.VMEM((depth // 2, width), out_weight.dtype)],
            [pltpu.SemaphoreType.DMA((2,))],
        )
        other = swap(stacked, "frame", frames // 2)
    cross, beside, own, token_late = call(
        functools.partial(late_kernel, tuned),
        "attend_far_late",
        (keep(query), keep(far1), keep(bias_far), *map(keep, state)),
        (row, row, row, token),
        [marks],
    )
    if tuned:
        early = [lax.ppermute(first, "head", [(2, 0), (1, 3)]), lax.ppermute(first, "head", [(3, 0), (0, 3)])]
        late = [lax.ppermute(cross, "head", [(3, 1), (0, 2)]), lax.ppermute(cross, "head", [(2, 1), (1, 2)])]
        late += [swap(beside, "head", 1)]
        other, came[1], *early, _ = gate([other, came[1], *early, token_late], "gate_early")
        shifts = (1, 3, 2)
        pieces = [came[1], swap(came[1], "frame", 1)]
        pieces += [stacked, other, swap(stacked, "frame", 1), swap(other, "frame", 1)]
    else:
        shifts = tuple(came)
        pieces = [piece for s in shifts for piece in (came[s], swap(came[s], "frame", 1))]
    (weight,) = call(
        functools.partial(assemble_kernel, tuned, shifts),
        "assemble_weight",
        (out_weight, *map(keep, pieces)),
        (pltpu.VMEM((heads, depth, width), jnp.bfloat16),),
        [],
    )
    if tuned:
        late = gate(late, "gate_late")
        *early, late3, late2, beside, weight = gate([*early, *late, weight], "gate_all")
        parts = [own, beside, *early, late2, late3]
    else:
        rows = jnp.concatenate([first, cross, beside, own]).reshape(heads, tokens // heads, HEAD_DIM)
        parts = [lax.dynamic_index_in_dim(rows, head, 0, False)]
        for s in range(1, heads):
            parts.append(swap(lax.dynamic_index_in_dim(rows, head ^ s, 0, False), "head", s))
    return project(tuned, parts, weight)


def solution(mesh):
    return jax.shard_map(
        on_device,
        mesh=mesh,
        in_specs=(
            P("frame", "head"),
            P("frame", "head"),
            P("frame", "head"),
            P("head", "frame", None, None),
            P("head", None),
        ),
        out_specs=P(("frame", "head"), None),
        check_vma=False,
    )
```

```python
import functools
import math

import jax
import jax.numpy as jnp
from jax import lax
from jax.experimental import pallas as pl
from jax.experimental.pallas import tpu as pltpu
from jax.sharding import PartitionSpec as P

HEAD_DIM = 128
TROWS = 4
TCOLS = 8
WIN = 45
TILE = 64
SPAN = TCOLS * TILE
HALF = SPAN // 2
KEYS = 6 * TILE
SHIFT = 2 * TILE
PAIR = 2 * SPAN
FAR = -(2.0**100)
RATE = math.log2(math.e) / math.sqrt(HEAD_DIM)
BIAS_SHAPE = (TROWS * 3 * SPAN, 128)
VMEM_BYTES = 10 * 1024 * 1024
GATE_FLOPS = 20_000_000_000


def keep(block):
    return pltpu.with_memory_space_constraint(block, pltpu.VMEM)


def stay(block):
    return pltpu.with_memory_space_constraint(block, pltpu.HBM)


def fill_bias(mask_ref, padded_ref, frame, frames, bias_refs):
    padded_ref[...] = jnp.zeros_like(padded_ref)
    padded_ref[: TROWS * TCOLS, :WIN] = mask_ref[...].astype(jnp.float32)
    turned = padded_ref[...].T
    key_col = lax.broadcasted_iota(jnp.int32, (TCOLS, 128), 0)
    step = key_col - lax.broadcasted_iota(jnp.int32, (TCOLS, 128), 1)
    odd = frame % 2
    for r in range(TROWS):
        windows = turned if r == 0 else pltpu.roll(turned, 128 - r * TCOLS, 1)
        for b in range(3):
            if not 0 <= r + b - 1 < TROWS:
                continue
            picked = []
            for a in range(3):
                base = 15 * a + 5 * b + 2
                chosen = jnp.zeros((TCOLS, 128), jnp.float32)
                for d in range(-2, 3):
                    chosen = jnp.where(step == d, jnp.broadcast_to(windows[base + d : base + d + 1, :], (TCOLS, 128)), chosen)
                picked.append(chosen > 0)
            own = picked[1] | (step == 0) if b == 1 else picked[1]
            low = jnp.where(picked[0] & (frame > 0), 0.0, FAR)
            high = jnp.where(picked[2] & (frame < frames - 1), 0.0, FAR)
            for ref, bias in zip(
                bias_refs,
                (jnp.where(own, 0.0, FAR), jnp.where(odd == 1, low, high), jnp.where(odd == 1, high, low)),
            ):
                for k in range(TCOLS):
                    start = (r * 3 + b) * SPAN + k * TILE
                    ref[start : start + TILE, :] = jnp.broadcast_to(bias[k : k + 1, :], (TILE, 128)).astype(
                        jnp.bfloat16
                    )


def fill_marks(marks_ref):
    tile = lax.broadcasted_iota(jnp.int32, (SPAN, 128), 0) // TILE
    lane = lax.broadcasted_iota(jnp.int32, (SPAN, 128), 1)
    marks_ref[...] = (lane == tile).astype(jnp.float32).astype(jnp.bfloat16)


def attend_blocks(blocks):
    def multiply(query, pieces):
        keys = jnp.concatenate([jnp.concatenate([key, bias], axis=1) for key, bias, _ in pieces], axis=0)
        return lax.dot_general(query, keys, (((1,), (1,)), ((), ())), preferred_element_type=jnp.float32)

    ahead = None
    for n, make in enumerate(blocks):
        query, pieces, before, store = make()
        scores = multiply(query, pieces) if ahead is None else ahead
        if n + 1 < len(blocks):
            ahead = multiply(*blocks[n + 1]()[:2])
        values = jnp.concatenate([value for _, _, value in pieces], axis=0)
        values = jnp.concatenate([values, jnp.ones_like(values)], axis=1)
        peak = jnp.max(scores, axis=1, keepdims=True)
        if before is not None:
            peak = jnp.maximum(peak, before[0][:, :1])
        expo = jnp.exp2((scores - peak) * RATE).astype(jnp.bfloat16)
        acc = jnp.dot(expo, values, preferred_element_type=jnp.float32)
        total, acc = acc[:, HEAD_DIM:], acc[:, :HEAD_DIM]
        if before is not None:
            fade = jnp.exp2((before[0] - peak) * RATE)
            total = total + fade * before[1]
            acc = acc + fade * before[2]
        store(peak, total, acc)


def flipped(row, flip, rows):
    return row + flip * (rows - 1 - 2 * row)


class Layout:
    def __init__(self, flip, q_ref, bias_ref, marks_ref):
        self.flip, self.q, self.bias, self.marks = flip, q_ref, bias_ref, marks_ref

    def query(self, row, side):
        at = pl.multiple_of(flipped(row, self.flip, TROWS) * SPAN + side * HALF, HALF)
        return jnp.concatenate([self.q[pl.ds(at, HALF), :], self.marks[side * HALF : (side + 1) * HALF, :]], axis=1)

    def piece(self, row, key_row, side, k_ref, v_ref, at_row):
        r, kr = flipped(row, self.flip, TROWS), flipped(key_row, self.flip, TROWS)
        at = pl.multiple_of((r * 3 + kr - r + 1) * SPAN + side * SHIFT, SHIFT)
        start = pl.multiple_of(at_row * SPAN + side * SHIFT, SHIFT)
        return (
            k_ref[pl.ds(start, KEYS), :],
            self.bias[pl.ds(at, KEYS), :],
            v_ref[pl.ds(start, KEYS), :],
        )


    def both(self, row, side, half0, half1):
        pieces = []
        for kr in around(row):
            half = (half0, half1)[kr // 2]
            pieces.append(self.piece(row, kr, side, half.at[0], half.at[1], flipped(kr % 2, self.flip, 2)))
        return pieces


def around(row):
    return range(max(row - 1, 0), min(row + 1, TROWS - 1) + 1)


def put(refs, at, state):
    for ref, value in zip(refs, state):
        ref[at : at + HALF, :] = jnp.broadcast_to(value, (HALF, 128))


def get(refs, at):
    return [ref[at : at + HALF, :] for ref in refs]


def flip_here(tuned):
    return (lax.axis_index("head") < lax.axis_size("head") // 2).astype(jnp.int32) if tuned else jnp.int32(0)


def start_all(copies):
    for copy in copies:
        copy.start()
    return copies


def pack_kernel(
    tuned, k_ref, v_ref, weight_ref, q_hbm, mask_hbm, first_ref, second_ref, mine_ref, less_ref, q_ref, mask_ref, sems
):
    flip = flip_here(tuned)
    half = mine_ref.shape[0]
    frame = lax.axis_index("frame")
    row = pl.multiple_of(frame % 2 * half, half)
    quarter = less_ref.shape[0]
    part = pl.multiple_of(row + frame // (lax.axis_size("frame") // 2) * quarter, quarter)
    moves = []
    for i, out in enumerate((first_ref, second_ref)):
        start = pl.multiple_of((flip if i == 0 else 1 - flip) * PAIR, PAIR)
        moves += [(source.at[pl.ds(start, PAIR)], out.at[j]) for j, source in enumerate((k_ref, v_ref))]
    moves += [(weight_ref.at[pl.ds(row, half)], mine_ref), (weight_ref.at[pl.ds(part, quarter)], less_ref), (q_hbm, q_ref), (mask_hbm, mask_ref)]
    for copy in start_all([pltpu.make_async_copy(a, b, sems.at[n]) for n, (a, b) in enumerate(moves)]):
        copy.wait()


def own_kernel(
    tuned,
    q_ref,
    mask_ref,
    half0,
    half1,
    again_ref,
    token_ref,
    peak,
    total,
    acc,
    bias_chip,
    bias_far,
    padded_ref,
    bias_ref,
    marks_ref,
    sem,
):
    token_ref[...] = jnp.zeros_like(token_ref)
    copy = pltpu.make_async_copy(half1, again_ref, sem)
    copy.start()
    fill_marks(marks_ref)
    fill_bias(
        mask_ref, padded_ref, lax.axis_index("frame"), lax.axis_size("frame"), (bias_ref, bias_chip, bias_far)
    )
    lay = Layout(flip_here(tuned), q_ref, bias_ref, marks_ref)
    blocks = []
    for row in range(TROWS):
        for side in range(2):
            blocks.append(
                lambda row=row, side=side: (
                    lay.query(row, side),
                    lay.both(row, side, half0, half1),
                    None,
                    lambda *state: put((peak, total, acc), row * SPAN + side * HALF, state),
                )
            )
    attend_blocks(blocks)
    copy.wait()


def chip_kernel(
    tuned, q_ref, near0, near1, bias_ref, peak_in, total_in, acc_in, peak, total, acc, token_ref, marks_ref
):
    token_ref[...] = jnp.zeros_like(token_ref)
    fill_marks(marks_ref)
    lay = Layout(flip_here(tuned), q_ref, bias_ref, marks_ref)
    blocks = []
    for row in range(TROWS):
        for side in range(2):
            blocks.append(
                lambda row=row, side=side, at=row * SPAN + side * HALF: (
                    lay.query(row, side),
                    lay.both(row, side, near0, near1),
                    get((peak_in, total_in, acc_in), at),
                    lambda *state: put((peak, total, acc), at, state),
                )
            )
    attend_blocks(blocks)


def finish(state):
    return (state[2] / state[1]).astype(jnp.bfloat16)


def early_kernel(
    tuned, q_ref, far0, bias_ref, peak_in, total_in, acc_in, out_ref, peak, total, acc, token_ref, marks_ref
):
    token_ref[...] = jnp.zeros_like(token_ref)
    fill_marks(marks_ref)
    for new, old in zip((peak, total, acc), (peak_in, total_in, acc_in)):
        new[PAIR:, :] = old[3 * SPAN :, :]
    lay = Layout(flip_here(tuned), q_ref, bias_ref, marks_ref)
    blocks = []
    for row in range(3):
        for side in range(2):

            def block(row=row, side=side, at=row * SPAN + side * HALF):
                def store(*state):
                    if row == 0:
                        out_ref[side * HALF : (side + 1) * HALF, :] = finish(state)
                    else:
                        put((peak, total, acc), at - SPAN, state)

                pieces = [
                    lay.piece(row, kr, side, far0.at[0], far0.at[1], flipped(kr, lay.flip, 2))
                    for kr in around(row)
                    if kr < 2
                ]
                return lay.query(row, side), pieces, get((peak_in, total_in, acc_in), at), store

            blocks.append(block)
    attend_blocks(blocks)


def late_kernel(
    tuned,
    q_ref,
    far_ref,
    bias_ref,
    peak_in,
    total_in,
    acc_in,
    cross_ref,
    near_ref,
    own_ref,
    token_ref,
    marks_ref,
):
    token_ref[...] = jnp.zeros_like(token_ref)
    fill_marks(marks_ref)
    lay = Layout(flip_here(tuned), q_ref, bias_ref, marks_ref)
    if tuned:
        head = lax.axis_index("head")
        beside = jnp.where((head == 0) | (head == lax.axis_size("head") - 1), 2, 3)
    else:
        beside = 2
    blocks = []
    for row, keys, out in ((1, (2,), cross_ref), (beside, (2, 3), near_ref), (5 - beside, (2, 3), own_ref)):
        for side in range(2):

            def block(row=row, keys=keys, out=out, side=side):
                def store(*state):
                    out[side * HALF : (side + 1) * HALF, :] = finish(state)

                pieces = [
                    lay.piece(row, kr, side, far_ref.at[0], far_ref.at[1], flipped(kr - 2, lay.flip, 2)) for kr in keys
                ]
                at = pl.multiple_of((row - 1) * SPAN + side * HALF, HALF)
                before = [ref[pl.ds(at, HALF), :] for ref in (peak_in, total_in, acc_in)]
                return lay.query(row, side), pieces, before, store

            blocks.append(block)
    attend_blocks(blocks)


def gate_kernel(*refs):
    pass


def stack_kernel(*refs):
    blocks, (out_ref, sems) = refs[:-3], refs[-2:]
    size = blocks[0].shape[0]
    copies = [
        pltpu.make_async_copy(block, out_ref.at[n * size : (n + 1) * size], sems.at[n]) for n, block in enumerate(blocks)
    ]
    for copy in start_all(copies):
        copy.wait()


def gate(blocks, name, flops=GATE_FLOPS):
    anywhere = pl.BlockSpec(memory_space=pl.ANY)
    return call(
        gate_kernel,
        name,
        [keep(block) for block in blocks],
        [pltpu.VMEM(block.shape, block.dtype) for block in blocks],
        [],
        [anywhere] * len(blocks),
        [anywhere] * len(blocks),
        [(n, n) for n in range(len(blocks))],
        flops,
    )


def call(kernel, name, ins, outs, scratch, specs=None, out_specs=None, aliases=(), flops=1_000_000):
    vmem = pl.BlockSpec(memory_space=pltpu.VMEM)
    return pl.pallas_call(
        kernel,
        out_shape=outs,
        in_specs=specs or [vmem] * len(ins),
        out_specs=tuple(out_specs or [vmem] * len(outs)),
        input_output_aliases=dict(aliases),
        scratch_shapes=scratch,
        compiler_params=pltpu.CompilerParams(vmem_limit_bytes=VMEM_BYTES),
        cost_estimate=pl.CostEstimate(flops=flops, bytes_accessed=1_000, transcendentals=0),
        name=name,
    )(*ins)


def assemble_kernel(tuned, shifts, own, *refs):
    pieces, whole = refs[:-1], refs[-1]
    frame, head = lax.axis_index("frame"), lax.axis_index("head")
    core = frame % 2
    half = own.shape[0] // 2
    whole[head] = own[...]

    def place(shift, row, piece):
        size = piece.shape[0]
        whole[head ^ shift, pl.ds(pl.multiple_of(row, size), size), :] = piece[...]

    for n, piece in enumerate(pieces[:2] if tuned else pieces):
        place(shifts[n // 2], (core if n % 2 == 0 else 1 - core) * half, piece)
    if tuned:
        quarter = half // 2
        y = frame // (lax.axis_size("frame") // 2)
        for n, piece in enumerate(pieces[2:]):
            row = (core ^ (n // 2)) * half + (y ^ (n % 2)) * quarter
            for m, shift in enumerate(shifts[1:]):
                place(shift, row, piece.at[m * quarter : (m + 1) * quarter])


def project_kernel(tuned, tile, *refs):
    parts, (weight_ref, out_hbm, out_ref, sems) = refs[:-4], refs[-4:]
    heads = weight_ref.shape[0]
    head = lax.axis_index("head")
    if tuned:
        own, near, early2, early3, late2, late3 = parts
        outer = (head == 0) | (head == heads - 1)
        blocks = [own[...], near[...], early2[...] + late2[...], early3[...] + late3[...]]
        first, second = jnp.where(outer, head ^ 2, head ^ 3), jnp.where(outer, head ^ 3, head ^ 2)
        order = [head, head ^ 1, first, second]
    else:
        blocks = [part[...] for part in parts]
        order = [head ^ s for s in range(heads)]
    rows = jnp.concatenate(blocks, axis=1)
    copies = []
    for n in range(weight_ref.shape[2] // tile):
        columns = slice(n * tile, (n + 1) * tile)
        weight = jnp.concatenate([weight_ref[h, :, columns] for h in order], axis=0)
        out_ref[:, columns] = jnp.dot(rows, weight, preferred_element_type=jnp.float32).astype(jnp.bfloat16)
        copies.append(pltpu.make_async_copy(out_ref.at[:, columns], out_hbm.at[:, columns], sems.at[n]))
        copies[-1].start()
    for copy in copies:
        copy.wait()


def project(tuned, parts, weight):
    tokens = parts[0].shape[0]
    heads, depth, width = weight.shape
    tile = 512
    vmem = pl.BlockSpec(memory_space=pltpu.VMEM)
    return pl.pallas_call(
        functools.partial(project_kernel, tuned, tile),
        out_shape=jax.ShapeDtypeStruct((tokens, width), jnp.bfloat16),
        in_specs=[vmem] * (len(parts) + 1),
        out_specs=pl.BlockSpec(memory_space=pltpu.HBM),
        scratch_shapes=[pltpu.VMEM((tokens, width), jnp.bfloat16), pltpu.SemaphoreType.DMA((width // tile,))],
        compiler_params=pltpu.CompilerParams(vmem_limit_bytes=VMEM_BYTES),
        name="project",
    )(*map(keep, parts), keep(weight))


def swap(block, axis, bit):
    return lax.ppermute(block, axis, [(i, i ^ bit) for i in range(lax.axis_size(axis))])


def on_device(queries, keys, values, block_mask, out_weight):
    frames = lax.axis_size("frame")
    heads = lax.axis_size("head")
    frame = lax.axis_index("frame")
    head = lax.axis_index("head")
    tuned = heads == TROWS
    mask = block_mask.reshape(TROWS * TCOLS, WIN)
    tokens = queries.shape[0]

    vmem, anywhere = pl.BlockSpec(memory_space=pltpu.VMEM), pl.BlockSpec(memory_space=pl.ANY)
    hbm = pl.BlockSpec(memory_space=pltpu.HBM)
    depth, width = out_weight.shape
    both = pltpu.VMEM((2, PAIR, HEAD_DIM), jnp.bfloat16)
    half0, half1, mine, less, query, mask = call(
        functools.partial(pack_kernel, tuned),
        "pack",
        (stay(keys), stay(values), stay(out_weight), stay(queries), stay(mask)),
        (
            both,
            both,
            pltpu.VMEM((depth // 2, width), out_weight.dtype),
            pltpu.VMEM((depth // 4, width), out_weight.dtype),
            pltpu.VMEM(queries.shape, queries.dtype),
            pltpu.VMEM(mask.shape, mask.dtype),
        ),
        [pltpu.SemaphoreType.DMA((8,))],
        [hbm] * 5,
    )
    links = [(i, i + 1) for i in range(1, frames - 1, 2)]
    links += [(j, i) for i, j in links]
    far0 = lax.ppermute(half0, "frame", links)
    near = [swap(block, "frame", 1) for block in (half0, half1)]

    if tuned:
        came = {3: swap(less, "head", 3), 1: swap(mine, "head", 1)}
    else:
        came = {s: swap(mine, "head", s) for s in range(1, heads)}

    marks = pltpu.VMEM((SPAN, 128), jnp.bfloat16)
    full = [pltpu.VMEM((tokens, 128), jnp.float32)] * 3
    three = [pltpu.VMEM((3 * SPAN, 128), jnp.float32)] * 3
    bias = pltpu.VMEM(BIAS_SHAPE, jnp.bfloat16)
    row = pltpu.VMEM((SPAN, HEAD_DIM), jnp.bfloat16)

    token = pltpu.VMEM((8, 128), jnp.float32)
    again, token_own, *state, bias_chip, bias_far = call(
        functools.partial(own_kernel, tuned),
        "attend_own",
        (keep(query), keep(mask), keep(half0), keep(half1)),
        (both, token, *full, bias, bias),
        [pltpu.VMEM((128, 128), jnp.float32), bias, marks, pltpu.SemaphoreType.DMA],
    )
    (far1,) = gate([lax.ppermute(again, "frame", links)], "gate_far")
    if tuned:
        came[3], _ = gate([came[3], token_own], "gate_own")
        came[2] = swap(came[3], "head", 1)
    *state, token_chip = call(
        functools.partial(chip_kernel, tuned),
        "attend_chip",
        (keep(query), *near, keep(bias_chip), *map(keep, state)),
        (*full, token),
        [marks],
    )
    if tuned:
        came[1], token_chip = gate([came[1], token_chip], "gate_middle")
        far0, _ = gate([far0, token_chip], "gate_halo")
    first, *state, token_early = call(
        functools.partial(early_kernel, tuned),
        "attend_far_early",
        (keep(query), far0, keep(bias_far), *map(keep, state)),
        (row, *three, token),
        [marks],
    )
    if tuned:
        (stacked,) = call(
            stack_kernel,
            "stack_weight",
            (keep(came[3]), keep(came[2]), token_early),
            [pltpu.VMEM((depth // 2, width), out_weight.dtype)],
            [pltpu.SemaphoreType.DMA((2,))],
        )
        other = swap(stacked, "frame", frames // 2)
    cross, beside, own, token_late = call(
        functools.partial(late_kernel, tuned),
        "attend_far_late",
        (keep(query), keep(far1), keep(bias_far), *map(keep, state)),
        (row, row, row, token),
        [marks],
    )
    if tuned:
        early = [lax.ppermute(first, "head", [(2, 0), (1, 3)]), lax.ppermute(first, "head", [(3, 0), (0, 3)])]
        late = [lax.ppermute(cross, "head", [(3, 1), (0, 2)]), lax.ppermute(cross, "head", [(2, 1), (1, 2)])]
        late += [swap(beside, "head", 1)]
        other, came[1], *early, _ = gate([other, came[1], *early, token_late], "gate_early")
        shifts = (1, 3, 2)
        pieces = [came[1], swap(came[1], "frame", 1)]
        pieces += [stacked, other, swap(stacked, "frame", 1), swap(other, "frame", 1)]
    else:
        shifts = tuple(came)
        pieces = [piece for s in shifts for piece in (came[s], swap(came[s], "frame", 1))]
    (weight,) = call(
        functools.partial(assemble_kernel, tuned, shifts),
        "assemble_weight",
        (out_weight, *map(keep, pieces)),
        (pltpu.VMEM((heads, depth, width), jnp.bfloat16),),
        [],
    )
    if tuned:
        late = gate(late, "gate_late")
        *early, late3, late2, beside, weight = gate([*early, *late, weight], "gate_all")
        parts = [own, beside, *early, late2, late3]
    else:
        rows = jnp.concatenate([first, cross, beside, own]).reshape(heads, tokens // heads, HEAD_DIM)
        parts = [lax.dynamic_index_in_dim(rows, head, 0, False)]
        for s in range(1, heads):
            parts.append(swap(lax.dynamic_index_in_dim(rows, head ^ s, 0, False), "head", s))
    return project(tuned, parts, weight)


def solution(mesh):
    return jax.shard_map(
        on_device,
        mesh=mesh,
        in_specs=(
            P("frame", "head"),
            P("frame", "head"),
            P("frame", "head"),
            P("head", "frame", None, None),
            P("head", None),
        ),
        out_specs=P(("frame", "head"), None),
        check_vma=False,
    )
```
